32 devices in a mesh: depth: 4 (over y, x), track: 8 (over z, core).
Axes of the slice: x: 2, y: 2, z: 4, core: 2. Of those that a mesh axis runs over, the one named last changes fastest.
Arguments:
- slowness_cells: float32 [128, 16384], P('depth'), may hold values from 0.5 to 2
- cell_of_group: int32 [128], P('track'), may hold values from 0 to 16383
- taper: float32 [256, 9], replicated, may hold values from 0 to 0.25
- secant: float32 [256], replicated, may hold values from 1 to 3
- primary: bfloat16 [128, 4096, 256], P('depth', 'track'), may hold values from -0.3984375 to 0.3984375
- quadrature: bfloat16 [128, 4096, 256], P('depth', 'track'), may hold values from -0.3984375 to 0.3984375
- observed: float32 [128, 4096], P('depth', 'track'), may hold values from -6 to 6
Outputs:
- focused: float32 [128, 4096], P('depth', 'track')
- gradient: float32 [128, 16384], P('depth')
The draws below stay inside these ranges and needn't reach their ends.
All inputs are finite; a program needn't handle non-finite values.
Results may differ from the reference program's by a relative error of at most 0.0003.
Values sent between devices are 32-bit elements; how exact they have to be, the bound alone decides.
No kernel may reach another device: no remote copies, remote signals or barrier semaphores. Data moves between devices by JAX's collectives and lax.ppermute only.
A program may use at most 128 MiB of HBM per device.

```python
import math
import jax
import jax.numpy as jnp
from jax import lax

ANGLES = 256
HALF_WIDTH = 4
NCELL = 16384
Z = 128
X = 4096
GROUPS = 128


def with_ends(values, own_key, low, high):
    extent = values.shape
    place = [jax.random.randint(jax.random.fold_in(own_key, axis), (), 0, extent[axis]) for axis in range(len(extent))]
    values = values.at[tuple(place)].set(low)
    longest = extent.index(max(extent))
    place[longest] = (place[longest] + 1) % extent[longest]
    return values.at[tuple(place)].set(high)


def block_scale(stream_key, extent, cuts, smallest, largest):
    def one(position, shards_of):
        draws = jax.random.uniform(jax.random.fold_in(jax.random.fold_in(stream_key, 6), position), (shards_of,), jnp.float32, smallest / len(cuts), largest / len(cuts))
        return jnp.repeat(jnp.exp(draws), extent[position] // shards_of).reshape((-1,) + (1,) * (len(extent) - position - 1))

    factor_of = one(*cuts[0])
    for cut in cuts[1:]:
        factor_of = factor_of * one(*cut)
    return factor_of


def gaussian(own_key, shape, scale, most, cuts=(), kind=jnp.bfloat16):
    loudness = block_scale(own_key, shape, cuts, -0.22, 0.18) if cuts else 1.0
    values = jax.random.normal(own_key, shape, jnp.float32) * scale * loudness
    return jnp.minimum(jnp.maximum(values, -most), most).astype(kind)


def setup_inputs(seed: int = 0) -> dict:
    streams_of = jax.random.split(jax.random.key(seed), 8)
    return {
        "slowness_cells": jnp.clip(jnp.exp(math.log(2.0) - 1.3862944 * jax.random.uniform(streams_of[0], (Z, NCELL), jnp.float32) ** block_scale(streams_of[0], (Z, NCELL), ((0, 4),), -0.2, 0.2)), 0.5, 2.0),
        "cell_of_group": with_ends(jax.random.randint(streams_of[1], (GROUPS,), 0, NCELL), jax.random.fold_in(streams_of[1], 1), 0, NCELL - 1).astype(jnp.int32),
        "taper": jnp.clip(jax.random.uniform(streams_of[2], (ANGLES, 2 * HALF_WIDTH + 1), jnp.float32, 0.0, 0.25), 0.0, 0.25),
        "secant": jnp.clip(jnp.exp(jax.random.uniform(streams_of[3], (ANGLES,), jnp.float32, math.log(1.0), math.log(3.0))), 1.0, 3.0),
        "primary": gaussian(streams_of[4], (Z, X, ANGLES), 0.0625, 0.3984375, ((0, 4), (1, 8))),
        "quadrature": gaussian(streams_of[5], (Z, X, ANGLES), 0.0625, 0.3984375, ((0, 4), (1, 8))),
        "observed": gaussian(streams_of[6], (Z, X), 1.0, 6.0, ((0, 4), (1, 8)), jnp.float32),
    }


OMEGA = 0.25


def reference(slowness_cells, cell_of_group, taper, secant, primary, quadrature, observed):
    taps = taper.shape[1]
    reach = (taps - 1) // 2
    traces = primary.shape[1]
    group = traces // cell_of_group.shape[0]
    cells = jnp.repeat(cell_of_group, group).astype(jnp.int32)
    slow = jnp.take(slowness_cells, cells, axis=1)
    padded = jnp.pad(slow, ((0, 0), (reach, reach)))
    high = lax.Precision.HIGHEST

    def forward(carry, items):
        row, prim, quad, seen = items
        window = jnp.stack([row[k:k + traces] for k in range(taps)], 0)
        increment = jnp.einsum('kx,ak->xa', window, taper, precision=high) * secant
        travel = carry + increment
        cosine = jnp.cos(OMEGA * travel)
        sine = jnp.sin(OMEGA * travel)
        prim = prim.astype(jnp.float32)
        quad = quad.astype(jnp.float32)
        image = jnp.sum(prim * cosine + quad * sine, axis=1)
        resid = image - seen
        time_grad = OMEGA * resid[:, None] * (quad * cosine - prim * sine)
        return travel, (image, time_grad)

    start = jnp.zeros((traces, taper.shape[0]), jnp.float32)
    _, (focused, time_grad) = lax.scan(forward, start, (padded, primary, quadrature, observed))

    def backward(carry, tgrad):
        step_grad = carry + tgrad
        spread = jnp.einsum('xa,ak->kx', step_grad * secant, taper, precision=high)
        spread = jnp.pad(spread, ((0, 0), (reach, reach)))
        total = jnp.zeros((traces,), jnp.float32)
        for k in range(taps):
            total = total + spread[k, 2 * reach - k:2 * reach - k + traces]
        return step_grad, total

    _, slow_grad = lax.scan(backward, start, time_grad, reverse=True)
    gradient = jax.ops.segment_sum(slow_grad.T, cells, num_segments=slowness_cells.shape[1]).T
    return focused, gradient
```

```python
import functools
import math

import jax
import jax.numpy as jnp
from jax import lax
from jax.experimental import pallas as pl
from jax.experimental.pallas import tpu as pltpu
from jax.sharding import PartitionSpec as P

OMEGA = 0.25
LANES = 128
SUBLANES = 8
MIB = 1024 * 1024
SINE = (4.442867755889893, -7.307443141937256, 3.594787359237671, -0.7843723297119141)
COSINE = (1.4142041206359863, -6.977642059326172, 5.71523904800415, -1.728348731994629)
HIGH = lax.Precision.HIGHEST
NT = (((1,), (1,)), ((), ()))
TN = (((0,), (0,)), ((), ()))
NN = (((1,), (0,)), ((), ()))


def dot32(a, b, dims):
    return lax.dot_general(a, b, dims, precision=HIGH, preferred_element_type=jnp.float32)


def dot16(a, b, dims):
    return lax.dot_general(a, b, dims, preferred_element_type=jnp.float32)


def iota(shape, dim):
    return lax.broadcasted_iota(jnp.int32, shape, dim)


def cos_sin_turns(t):
    r = t - jnp.round(t)
    z = r * r
    s = r * (SINE[0] + z * (SINE[1] + z * (SINE[2] + z * SINE[3])))
    c = COSINE[0] + z * (COSINE[1] + z * (COSINE[2] + z * COSINE[3]))
    return 1.0 - s * s, s * c


def split(x):
    hi = x.astype(jnp.bfloat16)
    return hi, (x - hi.astype(jnp.float32)).astype(jnp.bfloat16)


def gather_kernel(nloc, cells_ref, slow_ref, cum_ref, msg_ref, buf, sems):
    depth = slow_ref.shape[0]

    def copy(g):
        start = pl.multiple_of((cells_ref[g] // LANES) * LANES, LANES)
        return pltpu.make_async_copy(slow_ref.at[:, pl.ds(start, LANES)], buf.at[g], sems.at[g])

    for g in range(nloc):
        copy(g).start()
    lane = iota((depth, LANES), 1)
    lane1 = iota((1, LANES), 1)
    slow = jnp.zeros((depth, LANES), jnp.float32)
    ids = jnp.zeros((1, LANES), jnp.int32)
    for g in range(nloc):
        copy(g).wait()
        shift = lax.rem(g + LANES - lax.rem(cells_ref[g], LANES), LANES)
        slow = jnp.where(lane == g, pltpu.roll(buf[g], shift, 1), slow)
        ids = jnp.where(lane1 == g, cells_ref[g], ids)
    lower = (iota((depth, depth), 0) >= iota((depth, depth), 1)).astype(jnp.float32)
    cum = dot32(lower, slow, NN)
    cum_ref[...] = cum
    row = iota((SUBLANES, LANES), 0)
    col = iota((SUBLANES, LANES), 1)
    pick = jnp.where(((row == 2) & (col == 0)) | ((row == 3) & (col == nloc - 1)), 1.0, 0.0)
    ends = dot32(pick, cum, NT)
    ends = jnp.concatenate([ends, jnp.zeros((SUBLANES, LANES - depth), jnp.float32)], axis=1)
    total = jnp.broadcast_to(cum[depth - 1 : depth, :], (SUBLANES, LANES))
    idrow = jnp.broadcast_to(ids.astype(jnp.float32), (SUBLANES, LANES))
    msg_ref[...] = jnp.where(row == 0, total, jnp.where(row == 1, idrow, ends))


def main_kernel(
    nloc, group, reach, ndepth, ntrack, zb,
    m_ref, cum_ref, taper_ref, sec_ref, obs_ref, p_ref, q_ref,
    foc_ref, msg_ref, ids_ref,
    c_vmem, c_smem, ct, tab, cent_f, cent_e, edge_f, edge_o, edge_n, sem,
):
    depth, traces = obs_ref.shape
    taps = taper_ref.shape[1]
    angles = taper_ref.shape[0]
    step = pl.program_id(0)
    d, t = lax.axis_index("depth"), lax.axis_index("track")
    half = reach
    slots = 2 * reach

    @pl.when(step == 0)
    def _():
        slot = iota((2 * slots, taps), 0)
        k = iota((2 * slots, taps), 1)
        i = lax.rem(slot, slots)
        near = ((i < half) & (k < reach - i)) | ((i >= half) & (k >= 2 * reach - (i - half)))
        near = near.astype(jnp.float32)
        mask = jnp.where(slot < slots, 1.0 - near, near)
        weights = dot32(mask, taper_ref[...], NT) * sec_ref[...]
        tab[0 : 2 * slots, :] = weights
        tab[2 * slots : 4 * slots, :] = weights * (OMEGA / (2 * math.pi))
        tl, tr = jnp.maximum(t - 1, 0), jnp.minimum(t + 1, ntrack - 1)
        has_l = (t > 0).astype(jnp.float32)
        has_r = (t < ntrack - 1).astype(jnp.float32)
        above = jnp.zeros((1, LANES), jnp.float32)
        left = m_ref[d * ntrack + tl, 3:4, :]
        right = m_ref[d * ntrack + tr, 2:3, :]
        lane1 = iota((1, LANES), 1)
        for e in range(ndepth - 1):
            on = (e < d).astype(jnp.float32)
            above += on * m_ref[e * ntrack + t, 0:1, :]
            l_row = m_ref[e * ntrack + tl, 0:1, :]
            r_row = m_ref[e * ntrack + tr, 0:1, :]
            left += on * jnp.sum(jnp.where(lane1 == nloc - 1, l_row, 0.0), axis=1, keepdims=True)
            right += on * jnp.sum(jnp.where(lane1 == 0, r_row, 0.0), axis=1, keepdims=True)
        row = iota((SUBLANES, LANES), 0)
        col = iota((SUBLANES, LANES), 1)
        halo = jnp.where(row == 0, left * has_l, jnp.where(row == 1, right * has_r, 0.0))
        place = ((row == 0) & (col == 0)) | ((row == 1) & (col == nloc + 1))
        halo = dot32(halo, place.astype(jnp.float32), TN)[:depth]
        own = pltpu.roll(cum_ref[...] + above, 1, 1)
        lane = iota((depth, LANES), 1)
        c_ext = jnp.where((lane >= 1) & (lane <= nloc), own, halo)
        c_vmem[...] = c_ext
        copy = pltpu.make_async_copy(c_vmem, c_smem, sem)
        copy.start()
        pick = (iota((nloc, LANES), 1) == iota((nloc, LANES), 0) + 1).astype(jnp.float32)
        ct[:, 0:depth] = dot32(pick, c_ext, NT)
        ids = [m_ref[d * ntrack + s, 1:2, :] for s in range(ntrack)]
        ids_ref[...] = jnp.concatenate(ids, axis=0).astype(jnp.int32)
        copy.wait()

    own_w, near_w = tab[0:slots, :], tab[slots : 2 * slots, :]
    own_t, near_t = tab[2 * slots : 3 * slots, :], tab[3 * slots : 4 * slots, :]
    all_w = (own_w + near_w)[0:1, :]
    all_t = (own_t + near_t)[0:1, :]
    upper = iota((slots, 1), 0) < half
    lane = iota((slots, LANES), 1)
    mine = iota((nloc, traces), 0) == iota((nloc, traces), 1) // group

    def one(zi, carry):
        z = step * zb + zi
        column = jnp.where(iota((nloc, depth), 1) == z, ct[:, 0:depth], 0.0)
        c, s = cos_sin_turns(jnp.sum(column, axis=1, keepdims=True) * all_t)
        c_hi, c_lo = split(c)
        s_hi, s_lo = split(s)
        wc_hi, wc_lo = split(all_w * c)
        ws_hi, ws_lo = split(-all_w * s)
        rows_p = jnp.concatenate([c_hi, c_lo, ws_hi, ws_lo], axis=0)
        rows_q = jnp.concatenate([s_hi, s_lo, wc_hi, wc_lo], axis=0)
        both = dot16(rows_p, p_ref[zi], NT) + dot16(rows_q, q_ref[zi], NT)
        f = jnp.where(mine, both[0:nloc] + both[nloc : 2 * nloc], 0.0)
        e = jnp.where(mine, both[2 * nloc : 3 * nloc] + both[3 * nloc :], 0.0)
        cent_f[pl.ds(z, 1), :] = jnp.sum(f, axis=0, keepdims=True)
        cent_e[pl.ds(z, 1), :] = jnp.sum(e, axis=0, keepdims=True)
        here = lane == z
        for g in range(nloc):
            near = jnp.where(upper, c_smem[z, g], c_smem[z, g + 2])
            c, s = cos_sin_turns(own_t * c_smem[z, g + 1] + near_t * near)

            def edges(ref):
                first = ref[zi, g * group : g * group + 2 * SUBLANES, :].astype(jnp.float32)
                last = ref[zi, (g + 1) * group - 2 * SUBLANES : (g + 1) * group, :].astype(jnp.float32)
                return jnp.where(upper, first[:slots], last[2 * SUBLANES - slots :])

            p, q = edges(p_ref), edges(q_ref)
            f = p * c + q * s
            dd = q * c - p * s
            at = pl.ds(g * slots, slots)
            for ref, value in ((edge_f, f), (edge_o, dd * own_w), (edge_n, dd * near_w)):
                ref[at, :] = jnp.where(here, jnp.sum(value, axis=1, keepdims=True), ref[at, :])
        return carry

    @pl.when(step == 0)
    def _():
        for ref in (edge_f, edge_o, edge_n):
            ref[...] = jnp.zeros(ref.shape, jnp.float32)

    lax.fori_loop(0, zb, one, 0)

    @pl.when(step == pl.num_programs(0) - 1)
    def _():
        count = nloc * slots
        e, x = iota((count, traces), 0), iota((count, traces), 1)
        i = lax.rem(e, slots)
        spread = x == (e // slots) * group + jnp.where(i < half, i, group - slots + i)
        spread = spread.astype(jnp.float32)
        r = lax.rem(iota((depth, traces), 1), group)
        is_edge = (r < half) | (r >= group - half)
        f_x = dot32(edge_f[...], spread, TN)[:depth]
        o_x = dot32(edge_o[...], spread, TN)[:depth]
        n_x = dot32(edge_n[...], spread, TN)[:depth]
        focused = jnp.where(is_edge, f_x, cent_f[...])
        foc_ref[...] = focused
        resid = OMEGA * (focused - obs_ref[...])
        a = resid * jnp.where(is_edge, o_x, cent_e[...])
        b = resid * n_x
        x, lane_g = iota((traces, LANES), 0), iota((traces, LANES), 1)
        r, g = lax.rem(x, group), x // group
        to_own = (lane_g == g + 1).astype(jnp.float32)
        to_near = ((r < half) & (lane_g == g)) | ((r >= group - half) & (lane_g == g + 2))
        sums = dot32(a, to_own, NN) + dot32(b, to_near.astype(jnp.float32), NN)
        later = (iota((depth, depth), 1) >= iota((depth, depth), 0)).astype(jnp.float32)
        sums = dot32(later, sums, NN)
        parts = depth // SUBLANES
        width = LANES // parts
        lane8 = iota((SUBLANES, LANES), 1)
        packed = jnp.zeros((SUBLANES, LANES), jnp.float32)
        for part in range(parts):
            piece = sums[part * SUBLANES : (part + 1) * SUBLANES]
            piece = piece if part == 0 else pltpu.roll(piece, part * width, 1)
            packed = jnp.where(lane8 // width == part, piece, packed)
        msg_ref[...] = packed


def scatter_kernel(nloc, ndepth, ntrack, m_ref, ids_ref, out_ref):
    depth = out_ref.shape[0]
    d = lax.axis_index("depth")
    parts = depth // SUBLANES
    width = LANES // parts
    lane = iota((depth, LANES), 1)
    out_ref[...] = jnp.zeros(out_ref.shape, jnp.float32)

    def segment(s, carry):
        packed = m_ref[d * ntrack + s]
        pieces = [packed] + [pltpu.roll(packed, LANES - k * width, 1) for k in range(1, parts)]
        below = jnp.zeros((1, LANES), jnp.float32)
        for e in range(1, ndepth):
            below += (e > d).astype(jnp.float32) * m_ref[e * ntrack + s, 0:1, :]
        sums = jnp.concatenate(pieces, axis=0) + below
        for j in range(nloc + 2):
            if j == 0:
                cell, on = ids_ref[jnp.maximum(s - 1, 0), nloc - 1], s > 0
            elif j == nloc + 1:
                cell, on = ids_ref[jnp.minimum(s + 1, ntrack - 1), 0], s < ntrack - 1
            else:
                cell, on = ids_ref[s, j - 1], True
            at = lax.rem(cell, LANES)
            start = pl.multiple_of((cell // LANES) * LANES, LANES)
            moved = pltpu.roll(sums, lax.rem(at + LANES - j, LANES), 1)
            hit = lane == jnp.where(on, at, -1)
            out_ref[:, pl.ds(start, LANES)] += jnp.where(hit, moved, 0.0)
        return carry

    lax.fori_loop(0, ntrack, segment, 0)


def whole(shape):
    return pl.BlockSpec(shape, lambda *_: (0,) * len(shape))


def on_device(slowness_cells, cell_of_group, taper, secant, primary, quadrature, observed):
    ndepth, ntrack = lax.axis_size("depth"), lax.axis_size("track")
    ndev = ndepth * ntrack
    axes = ("depth", "track")
    angles, taps = taper.shape
    reach = (taps - 1) // 2
    slots = 2 * reach
    depth, traces, _ = primary.shape
    nloc = cell_of_group.shape[0]
    group = traces // nloc
    ncells = slowness_cells.shape[1]
    f32 = functools.partial(jax.ShapeDtypeStruct, dtype=jnp.float32)
    smem = pl.BlockSpec(memory_space=pltpu.SMEM)
    vmem = pl.BlockSpec(memory_space=pltpu.VMEM)
    hbm = pl.BlockSpec(memory_space=pl.ANY)

    cum, msg = pl.pallas_call(
        functools.partial(gather_kernel, nloc),
        out_shape=(f32((depth, LANES)), f32((SUBLANES, LANES))),
        in_specs=[smem, hbm],
        out_specs=(vmem, vmem),
        scratch_shapes=[pltpu.VMEM((nloc, depth, LANES), jnp.float32), pltpu.SemaphoreType.DMA((nloc,))],
        name="gather",
    )(cell_of_group, slowness_cells)
    msgs = lax.all_to_all(jnp.broadcast_to(msg[None], (ndev,) + msg.shape), axes, 0, 0)

    zb = 4
    block = pl.BlockSpec((zb, traces, angles), lambda i: (i, 0, 0))
    focused, sums, ids = pl.pallas_call(
        functools.partial(main_kernel, nloc, group, reach, ndepth, ntrack, zb),
        grid=(depth // zb,),
        out_shape=(
            f32((depth, traces)),
            f32((SUBLANES, LANES)),
            jax.ShapeDtypeStruct((ntrack, LANES), jnp.int32),
        ),
        in_specs=[
            whole(msgs.shape), whole(cum.shape), whole(taper.shape), whole((1, angles)),
            whole(observed.shape), block, block,
        ],
        out_specs=(whole((depth, traces)), whole((SUBLANES, LANES)), whole((ntrack, LANES))),
        scratch_shapes=[
            pltpu.VMEM((depth, LANES), jnp.float32),
            pltpu.SMEM((depth, LANES), jnp.float32),
            pltpu.VMEM((nloc, LANES), jnp.float32),
            pltpu.VMEM((4 * slots, angles), jnp.float32),
            pltpu.VMEM((depth, traces), jnp.float32),
            pltpu.VMEM((depth, traces), jnp.float32),
            pltpu.VMEM((nloc * slots, LANES), jnp.float32),
            pltpu.VMEM((nloc * slots, LANES), jnp.float32),
            pltpu.VMEM((nloc * slots, LANES), jnp.float32),
            pltpu.SemaphoreType.DMA,
        ],
        compiler_params=pltpu.CompilerParams(vmem_limit_bytes=40 * MIB),
        name="focus",
    )(msgs, cum, taper, secant.reshape(1, angles), observed, primary, quadrature)
    all_sums = lax.all_to_all(jnp.broadcast_to(sums[None], (ndev,) + sums.shape), axes, 0, 0)

    gradient = pl.pallas_call(
        functools.partial(scatter_kernel, nloc, ndepth, ntrack),
        out_shape=f32((depth, ncells)),
        in_specs=[vmem, smem],
        out_specs=vmem,
        compiler_params=pltpu.CompilerParams(vmem_limit_bytes=40 * MIB),
        name="scatter",
    )(all_sums, ids)
    return (focused, gradient)


def solution(mesh):
    in_specs = (
        P("depth", None),
        P("track"),
        P(),
        P(),
        P("depth", "track", None),
        P("depth", "track", None),
        P("depth", "track"),
    )
    out_specs = (P("depth", "track"), P("depth", None))
    return jax.shard_map(
        on_device, mesh=mesh, in_specs=in_specs, out_specs=out_specs, check_vma=False
    )
```

```python
import functools
import math

import jax
import jax.numpy as jnp
from jax import lax
from jax.experimental import pallas as pl
from jax.experimental.pallas import tpu as pltpu
from jax.sharding import PartitionSpec as P

OMEGA = 0.25
LANES = 128
SUBLANES = 8
MIB = 1024 * 1024
SINE = (4.442867755889893, -7.307443141937256, 3.594787359237671, -0.7843723297119141)
COSINE = (1.4142041206359863, -6.977642059326172, 5.71523904800415, -1.728348731994629)
HIGH = lax.Precision.HIGHEST
TURNS = OMEGA / (2 * math.pi)
NT = (((1,), (1,)), ((), ()))
TN = (((0,), (0,)), ((), ()))
NN = (((1,), (0,)), ((), ()))


def dot32(a, b, dims):
    return lax.dot_general(a, b, dims, precision=HIGH, preferred_element_type=jnp.float32)


def dot16(a, b, dims):
    return lax.dot_general(a, b, dims, preferred_element_type=jnp.float32)


def iota(shape, dim):
    return lax.broadcasted_iota(jnp.int32, shape, dim)


def cos_sin_turns(t):
    r = t - jnp.round(t)
    z = r * r
    s = r * (SINE[0] + z * (SINE[1] + z * (SINE[2] + z * SINE[3])))
    c = COSINE[0] + z * (COSINE[1] + z * (COSINE[2] + z * COSINE[3]))
    return 1.0 - s * s, s * c


def split(x):
    hi = x.astype(jnp.bfloat16)
    return hi, (x - hi.astype(jnp.float32)).astype(jnp.bfloat16)


def pack(rows, width):
    lane = iota((SUBLANES, LANES), 1)
    packed = rows[:SUBLANES]
    for part in range(1, rows.shape[0] // SUBLANES):
        piece = pltpu.roll(rows[part * SUBLANES : (part + 1) * SUBLANES], part * width, 1)
        packed = jnp.where(lane // width == part, piece, packed)
    return packed


def unpack(packed, parts):
    width = LANES // parts
    return jnp.concatenate([packed] + [pltpu.roll(packed, LANES - k * width, 1) for k in range(1, parts)], axis=0)


def pairs(count, first):
    swaps = [(i, i + 1) for i in range(first, count - 1, 2)]
    return swaps + [(j, i) for i, j in swaps]


def gather_kernel(nloc, ntrack, cells_ref, even_ref, odd_ref, slow_ref, cum_ref, msg_ref, buf, sems):
    depth = slow_ref.shape[0]
    t = lax.axis_index("track")
    even = lax.rem(t, 2) == 0
    left = jnp.where(even, odd_ref[nloc - 1], even_ref[nloc - 1])
    right = jnp.where(even, even_ref[0], odd_ref[0])
    cells = [left] + [cells_ref[g] for g in range(nloc)] + [right]

    def copy(j):
        start = pl.multiple_of((cells[j] // LANES) * LANES, LANES)
        return pltpu.make_async_copy(slow_ref.at[:, pl.ds(start, LANES)], buf.at[j], sems.at[j])

    for j in range(nloc + 2):
        copy(j).start()
    lane = iota((depth, LANES), 1)
    slow = jnp.zeros((depth, LANES), jnp.float32)
    for j in range(nloc + 2):
        copy(j).wait()
        shift = lax.rem(j + LANES - lax.rem(cells[j], LANES), LANES)
        slow = jnp.where(lane == j, pltpu.roll(buf[j], shift, 1), slow)
    first = (t == 0).astype(jnp.int32)
    last = (t < ntrack - 1).astype(jnp.int32)
    slow = jnp.where((lane >= first) & (lane < nloc + 1 + last), slow, 0.0)
    lower = (iota((depth, depth), 0) >= iota((depth, depth), 1)).astype(jnp.float32)
    cum = dot32(lower, slow, NN)
    cum_ref[...] = cum
    msg_ref[...] = jnp.broadcast_to(cum[depth - 1 :], msg_ref.shape)


def weight_rows(taper_ref, sec_ref, reach):
    taps, slots = taper_ref.shape[0], 2 * reach
    slot = iota((2 * slots, taps), 0)
    k = iota((2 * slots, taps), 1)
    i = lax.rem(slot, slots)
    near = ((i < reach) & (k < reach - i)) | ((i >= reach) & (k >= 2 * reach - (i - reach)))
    near = near.astype(jnp.float32)
    mask = jnp.where(slot < slots, 1.0 - near, near)
    weights = dot32(mask, taper_ref[...], NN) * sec_ref[...]
    return weights[:slots], weights[slots:]


def fetches(pairs, sems):
    copies = [pltpu.make_async_copy(source, target, sems.at[k]) for k, (source, target) in enumerate(pairs)]
    for copy in copies:
        copy.start()
    return copies


def focus_kernel(
    nloc, group, reach, count,
    *refs,
):
    totals = refs[: count - 1]
    (
        cells_ref, cum_hbm, taper_hbm, sec_hbm, obs_hbm, p_ref, q_ref,
        foc_ref, msg_ref,
        cum_ref, taper_ref, sec_ref, obs_ref, c_vmem, c_smem, b_ref, cent, edge_f, edge_o, edge_n,
        sem, small,
    ) = refs[count - 1 :]
    depth, traces = obs_ref.shape
    fetch = fetches(
        ((cum_hbm, cum_ref), (taper_hbm, taper_ref), (sec_hbm, sec_ref), (obs_hbm, obs_ref)), small
    )
    d = lax.axis_index("depth")
    slots = 2 * reach
    parts = depth // SUBLANES
    width = LANES // parts
    above = jnp.zeros((1, LANES), jnp.float32)
    for k, ref in enumerate(totals):
        above += ((d ^ (k + 1)) < d).astype(jnp.float32) * ref[0:1, :]
    for copy in fetch:
        copy.wait()
    c_ext = cum_ref[...] + above
    c_vmem[...] = c_ext
    copy = pltpu.make_async_copy(c_vmem, c_smem, sem)
    copy.start()
    own_w, near_w = weight_rows(taper_ref, sec_ref, reach)
    own_t, near_t = own_w * TURNS, near_w * TURNS
    all_w = (own_w + near_w)[0:1, :]
    all_t = all_w * TURNS
    upper = iota((slots, 1), 0) < reach
    lane_z = iota((depth, LANES), 1)

    def waves(g, carry):
        column = jnp.sum(jnp.where(lane_z == g + 1, c_ext, 0.0), axis=1, keepdims=True)
        c, s = cos_sin_turns(column * all_t)
        b_ref[g, 0] = jnp.concatenate(split(c) + split(-all_w * s), axis=0)
        b_ref[g, 1] = jnp.concatenate(split(s) + split(all_w * c), axis=0)
        return carry

    lax.fori_loop(0, nloc, waves, 0, unroll=4)
    col = lax.rem(iota((group, LANES), 1), depth)
    lane = iota((slots, LANES), 1)

    def one(g, carry):
        home = pl.ds(pl.multiple_of(g * group, group), group)
        out = jnp.zeros((group, LANES), jnp.float32)
        sums = [jnp.zeros((slots, LANES), jnp.float32)] * 3
        for first in range(0, depth, SUBLANES):
            at = pl.ds(first, SUBLANES)
            both = dot16(p_ref[at, home].reshape(SUBLANES * group, -1), b_ref[g, 0], NT)
            both += dot16(q_ref[at, home].reshape(SUBLANES * group, -1), b_ref[g, 1], NT)
            for z in range(first, first + SUBLANES):
                near = jnp.where(upper, c_smem[z, g], c_smem[z, g + 2])
                c, s = cos_sin_turns(own_t * c_smem[z, g + 1] + near_t * near)

                def rows(ref):
                    mine = ref[z, home]
                    low, high = mine[: 2 * SUBLANES].astype(jnp.float32), mine[group - 2 * SUBLANES :].astype(jnp.float32)
                    return jnp.where(upper, low[:slots], high[2 * SUBLANES - slots :])

                p, q = rows(p_ref), rows(q_ref)
                f = p * c + q * s
                dd = q * c - p * s
                values = (f, dd * own_w, dd * near_w)
                sums = [
                    jnp.where(lane == z, jnp.sum(value, axis=1, keepdims=True), old) for value, old in zip(values, sums)
                ]
            for z in range(first, first + SUBLANES):
                k = (z - first) * group
                out = jnp.where(col == z, both[k : k + group], out)
        cent[home, :] = out
        at = pl.ds(pl.multiple_of(g * slots, slots), slots)
        for ref, value in zip((edge_f, edge_o, edge_n), sums):
            ref[at, :] = value
        return carry

    copy.wait()
    lax.fori_loop(0, nloc, one, 0)

    gather = (iota((depth, LANES), 1) == iota((depth, LANES), 0)).astype(jnp.float32)
    count = nloc * slots
    e, x = iota((count, traces), 0), iota((count, traces), 1)
    i = lax.rem(e, slots)
    spread = (x == (e // slots) * group + jnp.where(i < reach, i, group - slots + i)).astype(jnp.float32)
    edge = jnp.concatenate([dot32(gather, ref[...], NT) for ref in (edge_f, edge_o, edge_n)], axis=0)
    edge = dot32(edge, spread, NN)
    r = lax.rem(iota((depth, traces), 1), group)
    is_edge = (r < reach) | (r >= group - reach)
    cent_t = jnp.transpose(cent[...])
    cent_f = cent_t[0:depth] + cent_t[depth : 2 * depth]
    cent_e = cent_t[2 * depth : 3 * depth] + cent_t[3 * depth :]
    focused = jnp.where(is_edge, edge[:depth], cent_f)
    foc_ref[...] = focused
    resid = OMEGA * (focused - obs_ref[...])
    a = resid * jnp.where(is_edge, edge[depth : 2 * depth], cent_e)
    b = resid * edge[2 * depth :]
    x, lane_g = iota((traces, LANES), 0), iota((traces, LANES), 1)
    r, g = lax.rem(x, group), x // group
    to_own = (lane_g == g + 1).astype(jnp.float32)
    to_near = ((r < reach) & (lane_g == g)) | ((r >= group - reach) & (lane_g == g + 2))
    sums = dot32(a, to_own, NN) + dot32(b, to_near.astype(jnp.float32), NN)
    later = (iota((depth, depth), 1) >= iota((depth, depth), 0)).astype(jnp.float32)
    tile = pack(dot32(later, sums, NN), width)
    row, lane8 = iota((SUBLANES, LANES), 0), iota((SUBLANES, LANES), 1)
    for g in range(nloc):
        at = (row == g % SUBLANES) & (lane8 == nloc + 2 + g // SUBLANES)
        tile = jnp.where(at, cells_ref[g].astype(jnp.float32), tile)
    msg_ref[...] = tile


def scatter_kernel(nloc, ndepth, ntrack, m_ref, out_ref, ids_vmem, ids_ref, sem):
    depth = out_ref.shape[0]
    d = lax.axis_index("depth")
    parts = depth // SUBLANES
    lane = iota((depth, LANES), 1)
    for s in range(ntrack):
        at = SUBLANES * s
        ids_vmem[at : at + SUBLANES, :] = m_ref[d * ntrack + s].astype(jnp.int32)
    copy = pltpu.make_async_copy(ids_vmem, ids_ref, sem)
    copy.start()
    out_ref[...] = jnp.zeros(out_ref.shape, jnp.float32)
    copy.wait()

    def cell_of(s, g):
        return ids_ref[SUBLANES * s + g % SUBLANES, nloc + 2 + g // SUBLANES]

    def segment(s, carry):
        below = jnp.zeros((1, LANES), jnp.float32)
        for e in range(1, ndepth):
            below += (e > d).astype(jnp.float32) * m_ref[e * ntrack + s, 0:1, :]
        sums = unpack(m_ref[d * ntrack + s], parts) + below
        for j in range(nloc + 2):
            if j == 0:
                cell, on = cell_of(jnp.maximum(s - 1, 0), nloc - 1), s > 0
            elif j == nloc + 1:
                cell, on = cell_of(jnp.minimum(s + 1, ntrack - 1), 0), s < ntrack - 1
            else:
                cell, on = cell_of(s, j - 1), True
            at = lax.rem(cell, LANES)
            start = pl.multiple_of((cell // LANES) * LANES, LANES)
            moved = pltpu.roll(sums, lax.rem(at + LANES - j, LANES), 1)
            hit = lane == jnp.where(on, at, -1)
            out_ref[:, pl.ds(start, LANES)] += jnp.where(hit, moved, 0.0)
        return carry

    lax.fori_loop(0, ntrack, segment, 0)


def whole(shape):
    return pl.BlockSpec(shape, lambda *_: (0,) * len(shape))


def on_device(slowness_cells, cell_of_group, taper, secant, primary, quadrature, observed):
    ndepth, ntrack = lax.axis_size("depth"), lax.axis_size("track")
    ndev = ndepth * ntrack
    axes = ("depth", "track")
    angles, taps = taper.shape
    reach = (taps - 1) // 2
    slots = 2 * reach
    depth, traces, _ = primary.shape
    nloc = cell_of_group.shape[0]
    group = traces // nloc
    ncells = slowness_cells.shape[1]
    f32 = functools.partial(jax.ShapeDtypeStruct, dtype=jnp.float32)
    smem = pl.BlockSpec(memory_space=pltpu.SMEM)
    vmem = pl.BlockSpec(memory_space=pltpu.VMEM)
    hbm = pl.BlockSpec(memory_space=pl.ANY)

    even = lax.ppermute(cell_of_group, "track", pairs(ntrack, 0))
    odd = lax.ppermute(cell_of_group, "track", pairs(ntrack, 1))
    cum, total = pl.pallas_call(
        functools.partial(gather_kernel, nloc, ntrack),
        out_shape=(f32((depth, LANES)), f32((SUBLANES, LANES))),
        in_specs=[smem, smem, smem, hbm],
        out_specs=(vmem, vmem),
        scratch_shapes=[
            pltpu.VMEM((nloc + 2, depth, LANES), jnp.float32),
            pltpu.SemaphoreType.DMA((nloc + 2,)),
        ],
        compiler_params=pltpu.CompilerParams(vmem_limit_bytes=4 * MIB),
        cost_estimate=pl.CostEstimate(flops=10**11, bytes_accessed=10**7, transcendentals=0),
        name="gather",
    )(cell_of_group, even, odd, slowness_cells)
    totals = [
        lax.ppermute(total, "depth", [(i, i ^ k) for i in range(ndepth)]) for k in range(1, ndepth)
    ]
    focused, sums = pl.pallas_call(
        functools.partial(focus_kernel, nloc, group, reach, ndepth),
        out_shape=(f32((depth, traces)), f32((SUBLANES, LANES))),
        in_specs=[vmem] * (ndepth - 1) + [smem] + [hbm] * 4 + [vmem] * 2,
        out_specs=(vmem, vmem),
        scratch_shapes=[
            pltpu.VMEM((depth, LANES), jnp.float32),
            pltpu.VMEM((taps, angles), jnp.float32),
            pltpu.VMEM((1, angles), jnp.float32),
            pltpu.VMEM((depth, traces), jnp.float32),
            pltpu.VMEM((depth, LANES), jnp.float32),
            pltpu.SMEM((depth, LANES), jnp.float32),
            pltpu.VMEM((nloc, 2, 4 * depth, angles), jnp.bfloat16),
            pltpu.VMEM((traces, LANES), jnp.float32),
            pltpu.VMEM((nloc * slots, LANES), jnp.float32),
            pltpu.VMEM((nloc * slots, LANES), jnp.float32),
            pltpu.VMEM((nloc * slots, LANES), jnp.float32),
            pltpu.SemaphoreType.DMA,
            pltpu.SemaphoreType.DMA((4,)),
        ],
        compiler_params=pltpu.CompilerParams(vmem_limit_bytes=20 * MIB),
        name="focus",
    )(*totals, cell_of_group, cum, taper.T, secant.reshape(1, angles), observed, primary, quadrature)
    all_sums = lax.all_to_all(jnp.broadcast_to(sums[None], (ndev,) + sums.shape), axes, 0, 0)

    gradient = pl.pallas_call(
        functools.partial(scatter_kernel, nloc, ndepth, ntrack),
        out_shape=f32((depth, ncells)),
        in_specs=[vmem],
        out_specs=vmem,
        scratch_shapes=[
            pltpu.VMEM((SUBLANES * ntrack, LANES), jnp.int32),
            pltpu.SMEM((SUBLANES * ntrack, LANES), jnp.int32),
            pltpu.SemaphoreType.DMA,
        ],
        compiler_params=pltpu.CompilerParams(vmem_limit_bytes=60 * MIB),
        name="scatter",
    )(all_sums)
    return (focused, gradient)


def solution(mesh):
    in_specs = (
        P("depth", None),
        P("track"),
        P(),
        P(),
        P("depth", "track", None),
        P("depth", "track", None),
        P("depth", "track"),
    )
    out_specs = (P("depth", "track"), P("depth", None))
    return jax.shard_map(
        on_device, mesh=mesh, in_specs=in_specs, out_specs=out_specs, check_vma=False
    )
```

```python
import functools
import math

import jax
import jax.numpy as jnp
from jax import lax
from jax.experimental import pallas as pl
from jax.experimental.pallas import tpu as pltpu
from jax.sharding import PartitionSpec as P

OMEGA = 0.25
LANES = 128
SUBLANES = 8
MIB = 1024 * 1024
SINE = (4.442867755889893, -7.307443141937256, 3.594787359237671, -0.7843723297119141)
COSINE = (1.4142041206359863, -6.977642059326172, 5.71523904800415, -1.728348731994629)
HIGH = lax.Precision.HIGHEST
TURNS = OMEGA / (2 * math.pi)
NT = (((1,), (1,)), ((), ()))
TN = (((0,), (0,)), ((), ()))
NN = (((1,), (0,)), ((), ()))


def dot32(a, b, dims):
    return lax.dot_general(a, b, dims, precision=HIGH, preferred_element_type=jnp.float32)


def dot16(a, b, dims):
    return lax.dot_general(a, b, dims, preferred_element_type=jnp.float32)


def iota(shape, dim):
    return lax.broadcasted_iota(jnp.int32, shape, dim)


def cos_sin_turns(t):
    r = t - jnp.round(t)
    z = r * r
    s = r * (SINE[0] + z * (SINE[1] + z * (SINE[2] + z * SINE[3])))
    c = COSINE[0] + z * (COSINE[1] + z * (COSINE[2] + z * COSINE[3]))
    return 1.0 - s * s, s * c


def split(x):
    hi = x.astype(jnp.bfloat16)
    return hi, (x - hi.astype(jnp.float32)).astype(jnp.bfloat16)


def pack(rows, width):
    lane = iota((SUBLANES, LANES), 1)
    packed = rows[:SUBLANES]
    for part in range(1, rows.shape[0] // SUBLANES):
        piece = pltpu.roll(rows[part * SUBLANES : (part + 1) * SUBLANES], part * width, 1)
        packed = jnp.where(lane // width == part, piece, packed)
    return packed


def unpack(packed, parts):
    width = LANES // parts
    return jnp.concatenate([packed] + [pltpu.roll(packed, LANES - k * width, 1) for k in range(1, parts)], axis=0)


def pairs(count, first):
    swaps = [(i, i + 1) for i in range(first, count - 1, 2)]
    return swaps + [(j, i) for i, j in swaps]


def gather_kernel(nloc, ntrack, cells_ref, even_ref, odd_ref, slow_ref, cum_ref, msg_ref, buf, sems):
    depth = slow_ref.shape[0]
    t = lax.axis_index("track")
    even = lax.rem(t, 2) == 0
    left = jnp.where(even, odd_ref[nloc - 1], even_ref[nloc - 1])
    right = jnp.where(even, even_ref[0], odd_ref[0])
    cells = [left] + [cells_ref[g] for g in range(nloc)] + [right]

    def copy(j):
        start = pl.multiple_of((cells[j] // LANES) * LANES, LANES)
        return pltpu.make_async_copy(slow_ref.at[:, pl.ds(start, LANES)], buf.at[j], sems.at[j])

    for j in range(nloc + 2):
        copy(j).start()
    lane = iota((depth, LANES), 1)
    slow = jnp.zeros((depth, LANES), jnp.float32)
    for j in range(nloc + 2):
        copy(j).wait()
        shift = lax.rem(j + LANES - lax.rem(cells[j], LANES), LANES)
        slow = jnp.where(lane == j, pltpu.roll(buf[j], shift, 1), slow)
    first = (t == 0).astype(jnp.int32)
    last = (t < ntrack - 1).astype(jnp.int32)
    slow = jnp.where((lane >= first) & (lane < nloc + 1 + last), slow, 0.0)
    lower = (iota((depth, depth), 0) >= iota((depth, depth), 1)).astype(jnp.float32)
    cum = dot32(lower, slow, NN)
    cum_ref[...] = cum
    msg_ref[...] = jnp.broadcast_to(cum[depth - 1 :], msg_ref.shape)


def weight_rows(taper_ref, sec_ref, reach):
    taps, slots = taper_ref.shape[0], 2 * reach
    slot = iota((2 * slots, taps), 0)
    k = iota((2 * slots, taps), 1)
    i = lax.rem(slot, slots)
    near = ((i < reach) & (k < reach - i)) | ((i >= reach) & (k >= 2 * reach - (i - reach)))
    near = near.astype(jnp.float32)
    mask = jnp.where(slot < slots, 1.0 - near, near)
    weights = dot32(mask, taper_ref[...], NN) * sec_ref[...]
    return weights[:slots], weights[slots:]


def fetches(pairs, sems):
    copies = [pltpu.make_async_copy(source, target, sems.at[k]) for k, (source, target) in enumerate(pairs)]
    for copy in copies:
        copy.start()
    return copies


def focus_kernel(
    nloc, group, reach, count,
    *refs,
):
    totals = refs[: count - 1]
    (
        cells_ref, cum_hbm, taper_hbm, sec_hbm, obs_hbm, p_ref, q_ref,
        foc_ref, msg_ref,
        cum_ref, taper_ref, sec_ref, obs_ref, c_vmem, c_smem, b_ref, cent, edge_f, edge_o, edge_n,
        sem, small,
    ) = refs[count - 1 :]
    depth, traces = obs_ref.shape
    fetch = fetches(
        ((cum_hbm, cum_ref), (taper_hbm, taper_ref), (sec_hbm, sec_ref), (obs_hbm, obs_ref)), small
    )
    d = lax.axis_index("depth")
    slots = 2 * reach
    parts = depth // SUBLANES
    width = LANES // parts
    above = jnp.zeros((1, LANES), jnp.float32)
    for k, ref in enumerate(totals):
        above += ((d ^ (k + 1)) < d).astype(jnp.float32) * ref[0:1, :]
    fetch[0].wait()
    c_ext = cum_ref[...] + above
    c_vmem[...] = c_ext
    copy = pltpu.make_async_copy(c_vmem, c_smem, sem)
    copy.start()
    fetch[1].wait()
    fetch[2].wait()
    own_w, near_w = weight_rows(taper_ref, sec_ref, reach)
    own_t, near_t = own_w * TURNS, near_w * TURNS
    all_w = (own_w + near_w)[0:1, :]
    all_t = all_w * TURNS
    upper = iota((slots, 1), 0) < reach
    lane_z = iota((depth, LANES), 1)

    def waves(g, carry):
        column = jnp.sum(jnp.where(lane_z == g + 1, c_ext, 0.0), axis=1, keepdims=True)
        c, s = cos_sin_turns(column * all_t)
        b_ref[g, 0] = jnp.concatenate(split(c) + split(-all_w * s), axis=0)
        b_ref[g, 1] = jnp.concatenate(split(s) + split(all_w * c), axis=0)
        return carry

    lax.fori_loop(0, nloc, waves, 0, unroll=4)
    col = lax.rem(iota((group, LANES), 1), depth)
    lane = iota((slots, LANES), 1)

    def one(g, carry):
        home = pl.ds(pl.multiple_of(g * group, group), group)
        out = jnp.zeros((group, LANES), jnp.float32)
        sums = [jnp.zeros((slots, LANES), jnp.float32)] * 3
        for first in range(0, depth, SUBLANES):
            at = pl.ds(first, SUBLANES)
            both = dot16(p_ref[at, home].reshape(SUBLANES * group, -1), b_ref[g, 0], NT)
            both += dot16(q_ref[at, home].reshape(SUBLANES * group, -1), b_ref[g, 1], NT)
            for z in range(first, first + SUBLANES):
                near = jnp.where(upper, c_smem[z, g], c_smem[z, g + 2])
                c, s = cos_sin_turns(own_t * c_smem[z, g + 1] + near_t * near)

                def rows(ref):
                    mine = ref[z, home]
                    low, high = mine[: 2 * SUBLANES].astype(jnp.float32), mine[group - 2 * SUBLANES :].astype(jnp.float32)
                    return jnp.where(upper, low[:slots], high[2 * SUBLANES - slots :])

                p, q = rows(p_ref), rows(q_ref)
                f = p * c + q * s
                dd = q * c - p * s
                values = (f, dd * own_w, dd * near_w)
                sums = [
                    jnp.where(lane == z, jnp.sum(value, axis=1, keepdims=True), old) for value, old in zip(values, sums)
                ]
            for z in range(first, first + SUBLANES):
                k = (z - first) * group
                out = jnp.where(col == z, both[k : k + group], out)
        cent[home, :] = out
        at = pl.ds(pl.multiple_of(g * slots, slots), slots)
        for ref, value in zip((edge_f, edge_o, edge_n), sums):
            ref[at, :] = value
        return carry

    copy.wait()
    lax.fori_loop(0, nloc, one, 0, unroll=2)

    gather = (iota((depth, LANES), 1) == iota((depth, LANES), 0)).astype(jnp.float32)
    count = nloc * slots
    e, x = iota((count, traces), 0), iota((count, traces), 1)
    i = lax.rem(e, slots)
    spread = (x == (e // slots) * group + jnp.where(i < reach, i, group - slots + i)).astype(jnp.float32)
    edge = jnp.concatenate([dot32(gather, ref[...], NT) for ref in (edge_f, edge_o, edge_n)], axis=0)
    edge = dot32(edge, spread, NN)
    r = lax.rem(iota((depth, traces), 1), group)
    is_edge = (r < reach) | (r >= group - reach)
    cent_t = jnp.transpose(cent[...])
    cent_f = cent_t[0:depth] + cent_t[depth : 2 * depth]
    cent_e = cent_t[2 * depth : 3 * depth] + cent_t[3 * depth :]
    focused = jnp.where(is_edge, edge[:depth], cent_f)
    foc_ref[...] = focused
    fetch[3].wait()
    resid = OMEGA * (focused - obs_ref[...])
    a = resid * jnp.where(is_edge, edge[depth : 2 * depth], cent_e)
    b = resid * edge[2 * depth :]
    x, lane_g = iota((traces, LANES), 0), iota((traces, LANES), 1)
    r, g = lax.rem(x, group), x // group
    to_own = (lane_g == g + 1).astype(jnp.float32)
    to_near = ((r < reach) & (lane_g == g)) | ((r >= group - reach) & (lane_g == g + 2))
    sums = dot32(a, to_own, NN) + dot32(b, to_near.astype(jnp.float32), NN)
    later = (iota((depth, depth), 1) >= iota((depth, depth), 0)).astype(jnp.float32)
    tile = pack(dot32(later, sums, NN), width)
    row, lane8 = iota((SUBLANES, LANES), 0), iota((SUBLANES, LANES), 1)
    for g in range(nloc):
        at = (row == g % SUBLANES) & (lane8 == nloc + 2 + g // SUBLANES)
        tile = jnp.where(at, cells_ref[g].astype(jnp.float32), tile)
    msg_ref[...] = tile


def scatter_kernel(nloc, ndepth, ntrack, m_ref, out_hbm, acc, ids_vmem, ids_ref, sem, out_sems):
    depth = acc.shape[1]
    d = lax.axis_index("depth")
    parts = depth // SUBLANES
    lane = iota((depth, LANES), 1)
    for s in range(ntrack):
        at = SUBLANES * s
        ids_vmem[at : at + SUBLANES, :] = m_ref[d * ntrack + s].astype(jnp.int32)
    copy = pltpu.make_async_copy(ids_vmem, ids_ref, sem)
    copy.start()
    acc[...] = jnp.zeros(acc.shape, jnp.float32)
    copy.wait()

    def cell_of(s, g):
        return ids_ref[SUBLANES * s + g % SUBLANES, nloc + 2 + g // SUBLANES]

    def sums_of(s):
        below = jnp.zeros((1, LANES), jnp.float32)
        for e in range(1, ndepth):
            below += (e > d).astype(jnp.float32) * m_ref[e * ntrack + s, 0:1, :]
        return unpack(m_ref[d * ntrack + s], parts) + below

    def two(pair, carry):
        segments = (2 * pair, 2 * pair + 1)
        sums = [sums_of(s) for s in segments]
        for j in range(nloc + 2):
            for k, s in enumerate(segments):
                if j == 0:
                    cell, on = cell_of(jnp.maximum(s - 1, 0), nloc - 1), s > 0
                elif j == nloc + 1:
                    cell, on = cell_of(jnp.minimum(s + 1, ntrack - 1), 0), s < ntrack - 1
                else:
                    cell, on = cell_of(s, j - 1), True
                at = lax.rem(cell, LANES)
                start = pl.multiple_of((cell // LANES) * LANES, LANES)
                moved = pltpu.roll(sums[k], lax.rem(at + LANES - j, LANES), 1)
                hit = lane == jnp.where(on, at, -1)
                acc[k, :, pl.ds(start, LANES)] += jnp.where(hit, moved, 0.0)
        return carry

    lax.fori_loop(0, ntrack // 2, two, 0)
    writes = []
    for part in range(parts):
        rows = pl.ds(part * SUBLANES, SUBLANES)
        acc[0, rows] += acc[1, rows]
        writes.append(pltpu.make_async_copy(acc.at[0, rows], out_hbm.at[rows], out_sems.at[part]))
        writes[-1].start()
    for write in writes:
        write.wait()


def on_device(slowness_cells, cell_of_group, taper, secant, primary, quadrature, observed):
    ndepth, ntrack = lax.axis_size("depth"), lax.axis_size("track")
    ndev = ndepth * ntrack
    axes = ("depth", "track")
    angles, taps = taper.shape
    reach = (taps - 1) // 2
    slots = 2 * reach
    depth, traces, _ = primary.shape
    nloc = cell_of_group.shape[0]
    group = traces // nloc
    ncells = slowness_cells.shape[1]
    f32 = functools.partial(jax.ShapeDtypeStruct, dtype=jnp.float32)
    smem = pl.BlockSpec(memory_space=pltpu.SMEM)
    vmem = pl.BlockSpec(memory_space=pltpu.VMEM)
    hbm = pl.BlockSpec(memory_space=pl.ANY)

    cells = pltpu.with_memory_space_constraint(cell_of_group, pltpu.HBM)
    even = lax.ppermute(cell_of_group, "track", pairs(ntrack, 0))
    odd = lax.ppermute(cell_of_group, "track", pairs(ntrack, 1))
    cum, total = pl.pallas_call(
        functools.partial(gather_kernel, nloc, ntrack),
        out_shape=(f32((depth, LANES)), f32((SUBLANES, LANES))),
        in_specs=[smem, smem, smem, hbm],
        out_specs=(vmem, vmem),
        scratch_shapes=[
            pltpu.VMEM((nloc + 2, depth, LANES), jnp.float32),
            pltpu.SemaphoreType.DMA((nloc + 2,)),
        ],
        compiler_params=pltpu.CompilerParams(vmem_limit_bytes=4 * MIB),
        cost_estimate=pl.CostEstimate(flops=10**11, bytes_accessed=10**7, transcendentals=0),
        name="gather",
    )(cells, even, odd, pltpu.with_memory_space_constraint(slowness_cells, pltpu.HBM))
    totals = [
        lax.ppermute(total, "depth", [(i, i ^ k) for i in range(ndepth)]) for k in range(1, ndepth)
    ]
    focused, sums = pl.pallas_call(
        functools.partial(focus_kernel, nloc, group, reach, ndepth),
        out_shape=(f32((depth, traces)), f32((SUBLANES, LANES))),
        in_specs=[vmem] * (ndepth - 1) + [smem] + [hbm] * 4 + [vmem] * 2,
        out_specs=(vmem, vmem),
        scratch_shapes=[
            pltpu.VMEM((depth, LANES), jnp.float32),
            pltpu.VMEM((taps, angles), jnp.float32),
            pltpu.VMEM((1, angles), jnp.float32),
            pltpu.VMEM((depth, traces), jnp.float32),
            pltpu.VMEM((depth, LANES), jnp.float32),
            pltpu.SMEM((depth, LANES), jnp.float32),
            pltpu.VMEM((nloc, 2, 4 * depth, angles), jnp.bfloat16),
            pltpu.VMEM((traces, LANES), jnp.float32),
            pltpu.VMEM((nloc * slots, LANES), jnp.float32),
            pltpu.VMEM((nloc * slots, LANES), jnp.float32),
            pltpu.VMEM((nloc * slots, LANES), jnp.float32),
            pltpu.SemaphoreType.DMA,
            pltpu.SemaphoreType.DMA((4,)),
        ],
        compiler_params=pltpu.CompilerParams(vmem_limit_bytes=20 * MIB),
        name="focus",
    )(*totals, cells, cum, taper.T, secant.reshape(1, angles), observed, primary, quadrature)
    all_sums = lax.all_to_all(jnp.broadcast_to(sums[None], (ndev,) + sums.shape), axes, 0, 0)

    gradient = pl.pallas_call(
        functools.partial(scatter_kernel, nloc, ndepth, ntrack),
        out_shape=f32((depth, ncells)),
        in_specs=[vmem],
        out_specs=hbm,
        scratch_shapes=[
            pltpu.VMEM((2, depth, ncells), jnp.float32),
            pltpu.VMEM((SUBLANES * ntrack, LANES), jnp.int32),
            pltpu.SMEM((SUBLANES * ntrack, LANES), jnp.int32),
            pltpu.SemaphoreType.DMA,
            pltpu.SemaphoreType.DMA((depth // SUBLANES,)),
        ],
        compiler_params=pltpu.CompilerParams(vmem_limit_bytes=60 * MIB),
        name="scatter",
    )(all_sums)
    return (focused, gradient)


def solution(mesh):
    in_specs = (
        P("depth", None),
        P("track"),
        P(),
        P(),
        P("depth", "track", None),
        P("depth", "track", None),
        P("depth", "track"),
    )
    out_specs = (P("depth", "track"), P("depth", None))
    return jax.shard_map(
        on_device, mesh=mesh, in_specs=in_specs, out_specs=out_specs, check_vma=False
    )
```
